512 devices in a mesh: walker: 32 (over y_hi, z, core), chol: 16 (over y_lo, x).
Axes of the slice: x: 4, y: 8 (y_hi: 2, y_lo: 4; y = y_hi * 4 + y_lo), z: 8, core: 2. Of those that a mesh axis runs over, the one named last changes fastest.
Arguments:
- chol_vectors: bfloat16 [256, 768, 192], P('chol', 'walker'), may hold values from -0.2 to 0.2, as said below
- green: bfloat16 [64, 768, 192], P('walker'), may hold values from -6 to 6
Outputs:
- energy: float32 [64], P('walker')
- gradient: float32 [64, 768, 192], P('walker', 'chol')
The draws below stay inside these ranges and needn't reach their ends.
Inputs may be any that keep to these rules, and one draw needn't show every extreme that they name: `chol_vectors`: independent entries of each vector; vector magnitudes differ from vector to vector.
All inputs are finite; a program needn't handle non-finite values.
Results may differ from the reference program's by a relative error of at most 0.0042.
Values may be sent and summed in bfloat16 or wider, within the bound.
No kernel may reach another device: no remote copies, remote signals or barrier semaphores. Data moves between devices by JAX's collectives and lax.ppermute only.
A program may use at most 64 MiB of HBM per device.

```python
import jax
import jax.numpy as jnp
from jax import lax

M = 768
NOCC = 192
NCHOL = 256
WALKERS = 64


def draw_chol_vectors(key, part):
    index = jnp.arange(NCHOL, dtype=jnp.float32) / (NCHOL - 1)
    decay = 3.0 ** (-0.5 * index)
    values = jax.random.normal(key, (NCHOL, M, NOCC), jnp.float32)
    values = values * M ** (-0.5) * decay[:, None, None]
    return jnp.clip(values, -0.19921875, 0.19921875).astype(jnp.bfloat16)


def block_levels(rng, shape, pieces, least, high):
    def one(dim, shards_of):
        steps = jax.random.uniform(jax.random.fold_in(jax.random.fold_in(rng, 6), dim), (shards_of,), jnp.float32, least / len(pieces), high / len(pieces))
        return jnp.repeat(jnp.exp(steps), shape[dim] // shards_of).reshape((-1,) + (1,) * (len(shape) - dim - 1))

    loudness = one(*pieces[0])
    for cut in pieces[1:]:
        loudness = loudness * one(*cut)
    return loudness


def normal_values(rng, dims, scale, bound, cuts=(), kind=jnp.bfloat16):
    array = jax.random.normal(rng, dims, jnp.float32) * scale
    if len(cuts) > 0:
        array = block_levels(rng, dims, cuts, -0.22, 0.18) * array
    return jnp.clip(array, min=-bound, max=bound).astype(kind)


def setup_inputs(seed: int = 0) -> dict:
    key_list = jax.random.split(jax.random.key(seed), 3)
    chol_vectors = draw_chol_vectors(jax.random.fold_in(key_list[2], 71), 0)
    green = normal_values(key_list[1], (WALKERS, M, NOCC), 1.0, 6.0, ((0, 32),))
    return dict(chol_vectors=chol_vectors, green=green)


def reference(chol_vectors, green):
    factors = chol_vectors.astype(jnp.float32)
    escale = 1.0 / (NCHOL * NOCC)
    gscale = 1.0 / (NCHOL ** 0.5)

    def one_walker(single):
        gfloat = single.astype(jnp.float32)
        tmat = jnp.einsum("kmi,mj->kij", factors, gfloat, precision=lax.Precision.HIGHEST)
        energy = jnp.sum(tmat * jnp.swapaxes(tmat, 1, 2)) * escale
        tround = lax.optimization_barrier(tmat.astype(jnp.bfloat16)).astype(jnp.float32)
        gradient = jnp.einsum("kmi,kji->mj", factors, tround, precision=lax.Precision.HIGHEST) * gscale
        return energy, gradient

    energy, gradient = lax.map(one_walker, green)
    return energy, gradient
```

```python
import jax
import jax.numpy as jnp
from jax import lax
from jax.experimental import pallas as pl
from jax.experimental.pallas import tpu as pltpu
from jax.sharding import Mesh
from jax.sharding import PartitionSpec as P

M = 768
NOCC = 192
NCHOL = 256
WALKER = ("y_hi", "z", "core")
CHOL = ("y_lo", "x")
PLACES = 16
KVEC = 16
ROWS = 24
WPER = 2
WIDE = KVEC * NOCC
CHUNK = 4 * NOCC
PAY = 160
VMEM_LIMIT = 56 * 1024 * 1024


def whole(shape=None):
    return pl.BlockSpec(memory_space=pltpu.VMEM)


def pack_kernel(chol_ref, out_ref):
    for k in range(0, KVEC, 2):
        pair = jnp.concatenate([chol_ref[k], chol_ref[k + 1]], axis=1)
        out_ref[:, k * NOCC : (k + 2) * NOCC] = pair


def pack(chol):
    return pl.pallas_call(
        pack_kernel,
        out_shape=jax.ShapeDtypeStruct((ROWS, WIDE), jnp.bfloat16),
        in_specs=[whole()],
        out_specs=whole(),
        name="pack",
    )(chol)


def split3(value):
    high = value.astype(jnp.bfloat16).astype(jnp.float32)
    left = value - high
    mid = left.astype(jnp.bfloat16).astype(jnp.float32)
    return high, mid, left - mid


def work_kernel(turn_ref, gt_ref, g_ref, own_ref, sib_ref, pay_ref, stack):
    half = PLACES * ROWS
    xs = (own_ref, sib_ref)
    for c in range(0, WIDE, CHUNK):
        part = jnp.dot(gt_ref[:, :half], own_ref[:, c : c + CHUNK], preferred_element_type=jnp.float32)
        part = part + jnp.dot(gt_ref[:, half:], sib_ref[:, c : c + CHUNK], preferred_element_type=jnp.float32)
        for q in range(CHUNK // NOCC):
            for w in range(WPER):
                tile = part[w * NOCC : (w + 1) * NOCC, q * NOCC : (q + 1) * NOCC]
                stack[w, c + q * NOCC : c + (q + 1) * NOCC, :] = tile.astype(jnp.bfloat16)
    straight = turn_ref[0] == 0
    terms = []
    energy = []
    for w in range(WPER):
        both = [jnp.dot(x[...], stack[w], preferred_element_type=jnp.float32) for x in xs]
        total = jnp.zeros((8, NOCC), jnp.float32)
        for s in range(2):
            green = g_ref[w, s * half : (s + 1) * half, :].astype(jnp.float32)
            total = total + (both[s] * green).reshape(half // 8, 8, NOCC).sum(axis=0)
        energy.append(jnp.sum(total))
        terms.append((jnp.where(straight, both[0], both[1]), jnp.where(straight, both[1], both[0])))
    row = lax.broadcasted_iota(jnp.int32, (16, 128), 0)
    carried = jnp.zeros((16, 128), jnp.float32)
    for w in range(WPER):
        filled = jnp.full((16, 128), energy[w], jnp.float32)
        for n, value in enumerate(split3(filled)):
            carried = jnp.where(row == 8 * w + n, value, carried)
    carried = carried.astype(jnp.bfloat16)
    for z in range(8):
        for y in range(2):
            block = z * 2 + y
            place = y * 8 + z
            here = [
                jnp.concatenate([low[block * ROWS : (block + 1) * ROWS], high[block * ROWS : (block + 1) * ROWS]], axis=0)
                for low, high in terms
            ]
            pay_ref[place, 0:48, :] = here[0][:, :128].astype(jnp.bfloat16)
            pay_ref[place, 48:96, :] = here[1][:, :128].astype(jnp.bfloat16)
            rest = jnp.concatenate([here[0][:, 128:], here[1][:, 128:]], axis=1)
            pay_ref[place, 96:144, :] = rest.astype(jnp.bfloat16)
            pay_ref[place, 144:160, :] = carried


def work(turn, gt, g, own, sib):
    return pl.pallas_call(
        work_kernel,
        out_shape=jax.ShapeDtypeStruct((PLACES, PAY, 128), jnp.bfloat16),
        in_specs=[pl.BlockSpec(memory_space=pltpu.SMEM)] + [whole()] * 4,
        out_specs=whole(),
        scratch_shapes=[pltpu.VMEM((WPER, WIDE, NOCC), jnp.bfloat16)],
        compiler_params=pltpu.CompilerParams(vmem_limit_bytes=VMEM_LIMIT),
        name="work",
    )(turn, gt, g, own, sib)


def close_kernel(got_ref, energy_ref, gradient_ref):
    escale = 1.0 / (NCHOL * NOCC)
    gscale = 1.0 / NCHOL**0.5
    total = got_ref[0].astype(jnp.float32)
    for n in range(1, PLACES):
        total = total + got_ref[n].astype(jnp.float32)
    for w in range(WPER):
        rest = total[96:144, 64 * w : 64 * (w + 1)]
        gradient_ref[w] = jnp.concatenate([total[48 * w : 48 * (w + 1)], rest], axis=1) * gscale
        base = 144 + 8 * w
        parts = total[base : base + 1] + total[base + 1 : base + 2] + total[base + 2 : base + 3]
        energy_ref[w] = parts[0, 0] * escale


def close(got):
    return pl.pallas_call(
        close_kernel,
        out_shape=(
            jax.ShapeDtypeStruct((WPER,), jnp.float32),
            jax.ShapeDtypeStruct((WPER, 48, NOCC), jnp.float32),
        ),
        in_specs=[whole()],
        out_specs=(pl.BlockSpec(memory_space=pltpu.SMEM), whole()),
        name="close",
    )(got)


def pairs(axis):
    return [(0, 1), (1, 0)]


def per_device(chol_vectors, green):
    y_hi = lax.axis_index("y_hi")
    core = lax.axis_index("core")
    packed = pack(chol_vectors)
    other = lax.ppermute(packed, "y_hi", pairs("y_hi"))
    first = jnp.where(y_hi == 0, packed, other)
    second = jnp.where(y_hi == 0, other, packed)
    mine = lax.all_gather(jnp.concatenate([first, second], axis=0), "z", axis=0, tiled=True)
    theirs = lax.ppermute(mine, "core", pairs("core"))
    split = green.reshape(WPER, 2, 8, 2, ROWS, NOCC)
    split = jnp.where(core == 0, split, jnp.flip(split, axis=3))
    g = split.transpose(0, 3, 2, 1, 4, 5).reshape(WPER, M, NOCC)
    gt = split.transpose(0, 5, 3, 2, 1, 4).reshape(WPER * NOCC, M)
    payload = work(core.reshape(1), gt, g, mine, theirs)
    got = lax.all_to_all(payload, CHOL, split_axis=0, concat_axis=0, tiled=True)
    return close(got)


def solution(mesh):
    torus = Mesh(
        mesh.devices.reshape(2, 8, 2, 4, 4),
        ("y_hi", "z", "core", "y_lo", "x"),
    )
    return jax.shard_map(
        per_device,
        mesh=torus,
        in_specs=(P(CHOL, WALKER, None), P(WALKER, None, None)),
        out_specs=(P(WALKER), P(WALKER, CHOL, None)),
        check_vma=False,
    )
```

```python
import jax
import jax.numpy as jnp
from jax import lax
from jax.experimental import pallas as pl
from jax.experimental.pallas import tpu as pltpu
from jax.sharding import Mesh
from jax.sharding import PartitionSpec as P

M = 768
NOCC = 192
NCHOL = 256
WALKER = ("y_hi", "z", "core")
CHOL = ("y_lo", "x")
ROWS = 24
BLOCK = 2 * ROWS
WPER = 2
QUARTER = 4
CHUNK = QUARTER * NOCC
DATA = 3 * BLOCK
CARRY = 16
VMEM_LIMIT = 40 * 1024 * 1024


def whole():
    return pl.BlockSpec(memory_space=pltpu.VMEM)


def pack_kernel(chol_ref, out_ref):
    for q in range(4):
        for k in range(0, QUARTER, 2):
            first = q * QUARTER + k
            pair = jnp.concatenate([chol_ref[first], chol_ref[first + 1]], axis=1)
            out_ref[q, :, k * NOCC : (k + 2) * NOCC] = pair


def pack(chol):
    return pl.pallas_call(
        pack_kernel,
        out_shape=jax.ShapeDtypeStruct((4, ROWS, CHUNK), jnp.bfloat16),
        in_specs=[whole()],
        out_specs=whole(),
        name="pack",
    )(chol)


def split3(value):
    high = value.astype(jnp.bfloat16).astype(jnp.float32)
    left = value - high
    mid = left.astype(jnp.bfloat16).astype(jnp.float32)
    return high, mid, left - mid


def carry(values):
    row = lax.broadcasted_iota(jnp.int32, (CARRY, 128), 0)
    out = jnp.zeros((CARRY, 128), jnp.float32)
    for n, value in enumerate(values):
        filled = jnp.broadcast_to(value, (CARRY, 128))
        for p, part in enumerate(split3(filled)):
            out = jnp.where(row == 3 * n + p, part, out)
    return out.astype(jnp.bfloat16)


def carried(rows, n):
    return rows[3 * n : 3 * n + 1] + rows[3 * n + 1 : 3 * n + 2] + rows[3 * n + 2 : 3 * n + 3]


def work_kernel(mine_ref, theirs_ref, own_ref, sib_ref, pay_ref, stack):
    side = lax.axis_index("y_hi")
    chunks = (own_ref, sib_ref)
    half = M // 2
    greens = (mine_ref, theirs_ref)
    for c, x_ref in enumerate(chunks):
        for g, green in enumerate(greens):
            part = jnp.dot(green[:, :half], x_ref[:, 0].reshape(half, CHUNK), preferred_element_type=jnp.float32)
            part = part + jnp.dot(green[:, half:], x_ref[:, 1].reshape(half, CHUNK), preferred_element_type=jnp.float32)
            for q in range(QUARTER):
                for w in range(WPER):
                    tile = part[w * NOCC : (w + 1) * NOCC, q * NOCC : (q + 1) * NOCC]
                    stack[c, g * WPER + w, q * NOCC : (q + 1) * NOCC, :] = tile.astype(jnp.bfloat16)
    diagonal = lax.broadcasted_iota(jnp.int32, (NOCC, NOCC), 0) == lax.broadcasted_iota(jnp.int32, (NOCC, NOCC), 1)
    energies = []
    for g, green in enumerate(greens):
        y = side if g == 0 else 1 - side
        traces = [jnp.zeros((NOCC, NOCC), jnp.float32) for _ in range(WPER)]
        for m in range(2):
            grads = []
            for w in range(WPER):
                n = g * WPER + w
                grad = jnp.dot(own_ref[:, m].reshape(half, CHUNK), stack[0, n], preferred_element_type=jnp.float32)
                grad = grad + jnp.dot(sib_ref[:, m].reshape(half, CHUNK), stack[1, n], preferred_element_type=jnp.float32)
                rounded = grad.astype(jnp.bfloat16)
                traces[w] = traces[w] + jnp.dot(
                    green[w * NOCC : (w + 1) * NOCC, m * half : (m + 1) * half], rounded, preferred_element_type=jnp.float32
                )
                grads.append(grad)
            rest = jnp.concatenate([grads[0][:, 128:], grads[1][:, 128:]], axis=1).astype(jnp.bfloat16)
            first, second = (grad[:, :128].astype(jnp.bfloat16) for grad in grads)
            for b in range(8):
                place = m * 8 + b
                x, y_lo = place % 4, place // 4
                base = y_lo * DATA
                rows = slice(b * BLOCK, (b + 1) * BLOCK)
                pay_ref[x, y, base : base + BLOCK, :] = first[rows]
                pay_ref[x, y, base + BLOCK : base + 2 * BLOCK, :] = second[rows]
                pay_ref[x, y, base + 2 * BLOCK : base + DATA, :] = rest[rows]
        energies = [jnp.sum(jnp.where(diagonal, trace, 0.0)) for trace in traces]
        rows = carry(energies)
        for x in range(4):
            pay_ref[x, y, 4 * DATA : 4 * DATA + CARRY, :] = rows


def work(mine, theirs, own, sib):
    return pl.pallas_call(
        work_kernel,
        out_shape=jax.ShapeDtypeStruct((4, 2, 4 * DATA + CARRY, 128), jnp.bfloat16),
        in_specs=[whole()] * 4,
        out_specs=whole(),
        scratch_shapes=[pltpu.VMEM((2, 2 * WPER, CHUNK, NOCC), jnp.bfloat16)],
        compiler_params=pltpu.CompilerParams(vmem_limit_bytes=VMEM_LIMIT),
        name="work",
    )(mine, theirs, own, sib)


def middle_kernel(got_ref, pay_ref):
    for y in range(2):
        total = got_ref[0, y].astype(jnp.float32)
        for x in range(1, 4):
            total = total + got_ref[x, y].astype(jnp.float32)
        rows = carry([carried(total[4 * DATA :], w)[:, :1] for w in range(WPER)])
        for y_lo in range(4):
            pay_ref[y * 4 + y_lo, :DATA, :] = total[y_lo * DATA : (y_lo + 1) * DATA].astype(jnp.bfloat16)
            pay_ref[y * 4 + y_lo, DATA:, :] = rows


def middle(got):
    return pl.pallas_call(
        middle_kernel,
        out_shape=jax.ShapeDtypeStruct((8, DATA + CARRY, 128), jnp.bfloat16),
        in_specs=[whole()],
        out_specs=whole(),
        name="middle",
    )(got)


def close_kernel(got_ref, energy_ref, gradient_ref):
    escale = 1.0 / (NCHOL * NOCC)
    gscale = 1.0 / NCHOL**0.5
    total = got_ref[0].astype(jnp.float32)
    for n in range(1, 8):
        total = total + got_ref[n].astype(jnp.float32)
    for w in range(WPER):
        rest = total[2 * BLOCK : DATA, 64 * w : 64 * (w + 1)]
        gradient_ref[w] = jnp.concatenate([total[BLOCK * w : BLOCK * (w + 1)], rest], axis=1) * gscale
        energy_ref[w] = carried(total[DATA:], w)[0, 0] * escale


def close(got):
    return pl.pallas_call(
        close_kernel,
        out_shape=(
            jax.ShapeDtypeStruct((WPER,), jnp.float32),
            jax.ShapeDtypeStruct((WPER, BLOCK, NOCC), jnp.float32),
        ),
        in_specs=[whole()],
        out_specs=(pl.BlockSpec(memory_space=pltpu.SMEM), whole()),
        name="close",
    )(got)


def swap(value, axis):
    return lax.ppermute(value, axis, [(0, 1), (1, 0)])


def exchange(value, axes):
    return lax.all_to_all(value, axes, split_axis=0, concat_axis=0, tiled=True)


def per_device(chol_vectors, green):
    packed = exchange(pack(chol_vectors), ("y_hi", "core"))
    turned = jnp.swapaxes(green, 1, 2).reshape(WPER * NOCC, M)
    packed, turned = lax.optimization_barrier((packed, turned))
    other = swap(turned, "y_hi")
    block = packed.reshape(2, BLOCK, CHUNK)
    own = exchange(jnp.broadcast_to(block[None], (8, *block.shape)), "z")
    own, other = lax.optimization_barrier((own, other))
    sib = swap(own, "core")
    payload = work(turned, other, own.reshape(8, 2, BLOCK, CHUNK), sib.reshape(8, 2, BLOCK, CHUNK))
    got = exchange(middle(exchange(payload, "x")), ("y_hi", "y_lo"))
    return close(got)


def solution(mesh):
    torus = Mesh(
        mesh.devices.reshape(2, 8, 2, 4, 4),
        ("y_hi", "z", "core", "y_lo", "x"),
    )
    return jax.shard_map(
        per_device,
        mesh=torus,
        in_specs=(P(CHOL, WALKER, None), P(WALKER, None, None)),
        out_specs=(P(WALKER), P(WALKER, CHOL, None)),
        check_vma=False,
    )
```

```python
import jax
import jax.numpy as jnp
from jax import lax
from jax.experimental import pallas as pl
from jax.experimental.pallas import tpu as pltpu
from jax.sharding import Mesh
from jax.sharding import PartitionSpec as P

M = 768
NOCC = 192
NCHOL = 256
WALKER = ("y_hi", "z", "core")
CHOL = ("y_lo", "x")
ROWS = 24
BLOCK = 2 * ROWS
WPER = 2
QUARTER = 4
CHUNK = QUARTER * NOCC
SHARE = WPER * NOCC // 4
NWALK = 2 * WPER
DATA = 3 * BLOCK
CARRY = 16
VMEM_LIMIT = 32 * 1024 * 1024
SMALL_LIMIT = 16 * 1024 * 1024


def whole():
    return pl.BlockSpec(memory_space=pltpu.VMEM)


def pack_kernel(chol_ref, out_ref):
    for q in range(4):
        for k in range(0, QUARTER, 2):
            first = q * QUARTER + k
            pair = jnp.concatenate([chol_ref[first], chol_ref[first + 1]], axis=1)
            out_ref[q, :, k * NOCC : (k + 2) * NOCC] = pair


def pack(chol):
    return pl.pallas_call(
        pack_kernel,
        out_shape=jax.ShapeDtypeStruct((4, ROWS, CHUNK), jnp.bfloat16),
        in_specs=[whole()],
        out_specs=whole(),
        compiler_params=pltpu.CompilerParams(vmem_limit_bytes=SMALL_LIMIT),
        name="pack",
    )(chol)


def split3(value):
    high = value.astype(jnp.bfloat16).astype(jnp.float32)
    left = value - high
    mid = left.astype(jnp.bfloat16).astype(jnp.float32)
    return high, mid, left - mid


def carry(values):
    row = lax.broadcasted_iota(jnp.int32, (CARRY, 128), 0)
    out = jnp.zeros((CARRY, 128), jnp.float32)
    for n, value in enumerate(values):
        filled = jnp.broadcast_to(value, (CARRY, 128))
        for p, part in enumerate(split3(filled)):
            out = jnp.where(row == 3 * n + p, part, out)
    return out.astype(jnp.bfloat16)


def carried(rows, n):
    return rows[3 * n : 3 * n + 1] + rows[3 * n + 1 : 3 * n + 2] + rows[3 * n + 2 : 3 * n + 3]


def contract(greens, x_ref, stack_ref, energy_ref):
    half = M // 2
    x = jnp.concatenate([x_ref[:, side].reshape(half, CHUNK) for side in range(2)], axis=0)
    diagonal = lax.broadcasted_iota(jnp.int32, (NOCC, NOCC), 0) == lax.broadcasted_iota(jnp.int32, (NOCC, NOCC), 1)
    for g, green in enumerate(greens):
        part = jnp.dot(green[...], x, preferred_element_type=jnp.float32)
        for w in range(WPER):
            n = g * WPER + w
            walker = part[w * NOCC : (w + 1) * NOCC]
            for q in range(QUARTER):
                stack_ref[n, q * NOCC : (q + 1) * NOCC, :] = walker[:, q * NOCC : (q + 1) * NOCC].astype(jnp.bfloat16)
            trace = jnp.dot(walker.astype(jnp.bfloat16), stack_ref[n], preferred_element_type=jnp.float32)
            value = jnp.sum(jnp.where(diagonal, trace, 0.0))
            energy_ref[n : n + 1, :] = jnp.full((1, 128), value, jnp.float32)


def first_kernel(mine_ref, s0_ref, s1_ref, s2_ref, s3_ref, x_ref, stack_ref, energy_ref, other_ref):
    here = lax.axis_index("x")
    for step, piece in enumerate((s0_ref, s1_ref, s2_ref, s3_ref)):
        base = lax.rem(here + step, 4) * SHARE
        other_ref[pl.ds(pl.multiple_of(base, 16), SHARE), :] = piece[...]
    contract((mine_ref, other_ref), x_ref, stack_ref, energy_ref)


def second_kernel(mine_ref, other_ref, x_ref, stack_ref, energy_ref):
    contract((mine_ref, other_ref), x_ref, stack_ref, energy_ref)


def params():
    return pltpu.CompilerParams(vmem_limit_bytes=VMEM_LIMIT)


STACKED = (
    jax.ShapeDtypeStruct((NWALK, CHUNK, NOCC), jnp.bfloat16),
    jax.ShapeDtypeStruct((NWALK, 128), jnp.float32),
)


def first(*args):
    return pl.pallas_call(
        first_kernel,
        out_shape=(*STACKED, jax.ShapeDtypeStruct((WPER * NOCC, M), jnp.bfloat16)),
        in_specs=[whole()] * len(args),
        out_specs=(whole(),) * 3,
        compiler_params=params(),
        name="first",
    )(*args)


def second(*args):
    return pl.pallas_call(
        second_kernel,
        out_shape=STACKED,
        in_specs=[whole()] * len(args),
        out_specs=(whole(),) * 2,
        compiler_params=params(),
        name="second",
    )(*args)


def spread_kernel(own_ref, sib_ref, stack0_ref, stack1_ref, e0_ref, e1_ref, pay_ref):
    side = lax.axis_index("y_hi")
    half = M // 2
    energies = e0_ref[...] + e1_ref[...]
    for g in range(2):
        y = side if g == 0 else 1 - side
        for m in range(2):
            grads = []
            for w in range(WPER):
                n = g * WPER + w
                grad = jnp.dot(own_ref[:, m].reshape(half, CHUNK), stack0_ref[n], preferred_element_type=jnp.float32)
                grads.append(
                    grad + jnp.dot(sib_ref[:, m].reshape(half, CHUNK), stack1_ref[n], preferred_element_type=jnp.float32)
                )
            rest = jnp.concatenate([grads[0][:, 128:], grads[1][:, 128:]], axis=1).astype(jnp.bfloat16)
            parts = [grad[:, :128].astype(jnp.bfloat16) for grad in grads] + [rest]
            for b in range(8):
                x, y_lo = b % 4, m * 2 + b // 4
                for p, part in enumerate(parts):
                    base = y_lo * DATA + p * BLOCK
                    pay_ref[x, y, base : base + BLOCK, :] = part[b * BLOCK : (b + 1) * BLOCK]
        rows = carry([energies[g * WPER + w : g * WPER + w + 1, :1] for w in range(WPER)])
        for x in range(4):
            pay_ref[x, y, 4 * DATA : 4 * DATA + CARRY, :] = rows


def spread(*args):
    return pl.pallas_call(
        spread_kernel,
        out_shape=jax.ShapeDtypeStruct((4, 2, 4 * DATA + CARRY, 128), jnp.bfloat16),
        in_specs=[whole()] * len(args),
        out_specs=whole(),
        compiler_params=params(),
        name="spread",
    )(*args)


def middle_kernel(got_ref, pay_ref):
    for y in range(2):
        total = got_ref[0, y].astype(jnp.float32)
        for x in range(1, 4):
            total = total + got_ref[x, y].astype(jnp.float32)
        rows = carry([carried(total[4 * DATA :], w)[:, :1] for w in range(WPER)])
        for y_lo in range(4):
            pay_ref[y * 4 + y_lo, :DATA, :] = total[y_lo * DATA : (y_lo + 1) * DATA].astype(jnp.bfloat16)
            pay_ref[y * 4 + y_lo, DATA:, :] = rows


def middle(*args):
    return pl.pallas_call(
        middle_kernel,
        out_shape=jax.ShapeDtypeStruct((8, DATA + CARRY, 128), jnp.bfloat16),
        in_specs=[whole()] * len(args),
        out_specs=whole(),
        compiler_params=pltpu.CompilerParams(vmem_limit_bytes=SMALL_LIMIT),
        name="middle",
    )(*args)


def close_kernel(got_ref, energy_ref, gradient_ref):
    escale = 1.0 / (NCHOL * NOCC)
    gscale = 1.0 / NCHOL**0.5
    total = got_ref[0].astype(jnp.float32)
    for n in range(1, 8):
        total = total + got_ref[n].astype(jnp.float32)
    for w in range(WPER):
        rest = total[2 * BLOCK : DATA, 64 * w : 64 * (w + 1)]
        gradient_ref[w] = jnp.concatenate([total[BLOCK * w : BLOCK * (w + 1)], rest], axis=1) * gscale
        energy_ref[w] = carried(total[DATA:], w)[0, 0] * escale


def close(got):
    return pl.pallas_call(
        close_kernel,
        out_shape=(
            jax.ShapeDtypeStruct((WPER,), jnp.float32),
            jax.ShapeDtypeStruct((WPER, BLOCK, NOCC), jnp.float32),
        ),
        in_specs=[whole()],
        out_specs=(pl.BlockSpec(memory_space=pltpu.SMEM), whole()),
        compiler_params=pltpu.CompilerParams(vmem_limit_bytes=SMALL_LIMIT),
        name="close",
    )(got)


def swap(value, axis):
    return lax.ppermute(value, axis, [(0, 1), (1, 0)])


def exchange(value, axes):
    return lax.all_to_all(value, axes, split_axis=0, concat_axis=0, tiled=True)


def per_device(chol_vectors, green):
    turned = jnp.swapaxes(green, 1, 2).reshape(WPER * NOCC, M)
    share = lax.dynamic_index_in_dim(turned.reshape(4, SHARE, M), lax.axis_index("x"), 0, keepdims=False)
    packed = exchange(pack(chol_vectors), ("y_hi", "core"))
    packed, share = lax.optimization_barrier((packed, share))
    share = swap(share, "y_hi")
    shares = [share] + [lax.ppermute(share, "x", [((x + step) % 4, x) for x in range(4)]) for step in (1, 2, 3)]
    block = packed.reshape(2, BLOCK, CHUNK)
    own = exchange(jnp.broadcast_to(block[None], (8, *block.shape)), "z")
    own, shares = lax.optimization_barrier((own, shares))
    sib = swap(own, "core")
    own, sib = (value.reshape(8, 2, BLOCK, CHUNK) for value in (own, sib))
    stack0, e0, other = first(turned, *shares, own)
    stack1, e1 = second(turned, other, sib)
    got = exchange(middle(exchange(spread(own, sib, stack0, stack1, e0, e1), "x")), ("y_hi", "y_lo"))
    return close(got)


def solution(mesh):
    torus = Mesh(
        mesh.devices.reshape(2, 8, 2, 4, 4),
        ("y_hi", "z", "core", "y_lo", "x"),
    )
    return jax.shard_map(
        per_device,
        mesh=torus,
        in_specs=(P(CHOL, WALKER, None), P(WALKER, None, None)),
        out_specs=(P(WALKER), P(WALKER, CHOL, None)),
        check_vma=False,
    )
```

```python
import jax
import jax.numpy as jnp
from jax import lax
from jax.experimental import pallas as pl
from jax.experimental.pallas import tpu as pltpu
from jax.sharding import Mesh
from jax.sharding import PartitionSpec as P

M = 768
NOCC = 192
NCHOL = 256
WALKER = ("y_hi", "z", "core")
CHOL = ("y_lo", "x")
ROWS = 24
BLOCK = 2 * ROWS
WPER = 2
QUARTER = 4
CHUNK = QUARTER * NOCC
SHARE = WPER * NOCC // 4
NWALK = 2 * WPER
DATA = 3 * BLOCK
CARRY = 16
VMEM_LIMIT = 32 * 1024 * 1024
SMALL_LIMIT = 16 * 1024 * 1024


def whole():
    return pl.BlockSpec(memory_space=pltpu.VMEM)


def fan_kernel(in_ref, out_ref):
    for n in range(4):
        for k in range(0, QUARTER, 2):
            pair = jnp.concatenate([in_ref[n, k], in_ref[n, k + 1]], axis=1)
            for z in range(8):
                out_ref[z, n, :, k * NOCC : (k + 2) * NOCC] = pair


def fan(quarters):
    return pl.pallas_call(
        fan_kernel,
        out_shape=jax.ShapeDtypeStruct((8, 4, ROWS, CHUNK), jnp.bfloat16),
        in_specs=[whole()],
        out_specs=whole(),
        compiler_params=pltpu.CompilerParams(vmem_limit_bytes=SMALL_LIMIT),
        name="fan",
    )(quarters)


def split3(value):
    high = value.astype(jnp.bfloat16).astype(jnp.float32)
    left = value - high
    mid = left.astype(jnp.bfloat16).astype(jnp.float32)
    return high, mid, left - mid


def carry(values):
    row = lax.broadcasted_iota(jnp.int32, (CARRY, 128), 0)
    out = jnp.zeros((CARRY, 128), jnp.float32)
    for n, value in enumerate(values):
        filled = jnp.broadcast_to(value, (CARRY, 128))
        for p, part in enumerate(split3(filled)):
            out = jnp.where(row == 3 * n + p, part, out)
    return out.astype(jnp.bfloat16)


def carried(rows, n):
    return rows[3 * n : 3 * n + 1] + rows[3 * n + 1 : 3 * n + 2] + rows[3 * n + 2 : 3 * n + 3]


def contract(greens, x_ref, stack_ref, energy_ref):
    half = M // 2
    x = jnp.concatenate([x_ref[:, side].reshape(half, CHUNK) for side in range(2)], axis=0)
    diagonal = lax.broadcasted_iota(jnp.int32, (NOCC, NOCC), 0) == lax.broadcasted_iota(jnp.int32, (NOCC, NOCC), 1)
    for g, green in enumerate(greens):
        part = jnp.dot(green[...], x, preferred_element_type=jnp.float32)
        for w in range(WPER):
            n = g * WPER + w
            walker = part[w * NOCC : (w + 1) * NOCC]
            for q in range(QUARTER):
                stack_ref[n, q * NOCC : (q + 1) * NOCC, :] = walker[:, q * NOCC : (q + 1) * NOCC].astype(jnp.bfloat16)
            trace = jnp.dot(walker.astype(jnp.bfloat16), stack_ref[n], preferred_element_type=jnp.float32)
            value = jnp.sum(jnp.where(diagonal, trace, 0.0))
            energy_ref[n : n + 1, :] = jnp.full((1, 128), value, jnp.float32)


def products_kernel(mine_ref, other_ref, x_ref, stack_ref, energy_ref):
    contract((mine_ref, other_ref), x_ref, stack_ref, energy_ref)


def params():
    return pltpu.CompilerParams(vmem_limit_bytes=VMEM_LIMIT)


STACKED = (
    jax.ShapeDtypeStruct((NWALK, CHUNK, NOCC), jnp.bfloat16),
    jax.ShapeDtypeStruct((NWALK, 128), jnp.float32),
)


def products(*args):
    return pl.pallas_call(
        products_kernel,
        out_shape=STACKED,
        in_specs=[whole()] * len(args),
        out_specs=(whole(),) * 2,
        compiler_params=params(),
        name="products",
    )(*args)


def spread_kernel(own_ref, sib_ref, stack0_ref, stack1_ref, e0_ref, e1_ref, pay_ref):
    side = lax.axis_index("y_hi")
    half = M // 2
    energies = e0_ref[...] + e1_ref[...]
    for g in range(2):
        y = side if g == 0 else 1 - side
        for m in range(2):
            grads = []
            for w in range(WPER):
                n = g * WPER + w
                grad = jnp.dot(own_ref[:, m].reshape(half, CHUNK), stack0_ref[n], preferred_element_type=jnp.float32)
                grads.append(
                    grad + jnp.dot(sib_ref[:, m].reshape(half, CHUNK), stack1_ref[n], preferred_element_type=jnp.float32)
                )
            rest = jnp.concatenate([grads[0][:, 128:], grads[1][:, 128:]], axis=1).astype(jnp.bfloat16)
            parts = [grad[:, :128].astype(jnp.bfloat16) for grad in grads] + [rest]
            for b in range(8):
                x, y_lo = b % 4, m * 2 + b // 4
                for p, part in enumerate(parts):
                    base = y_lo * DATA + p * BLOCK
                    pay_ref[x, y, base : base + BLOCK, :] = part[b * BLOCK : (b + 1) * BLOCK]
        rows = carry([energies[g * WPER + w : g * WPER + w + 1, :1] for w in range(WPER)])
        for x in range(4):
            pay_ref[x, y, 4 * DATA : 4 * DATA + CARRY, :] = rows


def spread(*args):
    return pl.pallas_call(
        spread_kernel,
        out_shape=jax.ShapeDtypeStruct((4, 2, 4 * DATA + CARRY, 128), jnp.bfloat16),
        in_specs=[whole()] * len(args),
        out_specs=whole(),
        compiler_params=params(),
        name="spread",
    )(*args)


def middle_kernel(got_ref, pay_ref):
    for y in range(2):
        total = got_ref[0, y].astype(jnp.float32)
        for x in range(1, 4):
            total = total + got_ref[x, y].astype(jnp.float32)
        rows = carry([carried(total[4 * DATA :], w)[:, :1] for w in range(WPER)])
        for y_lo in range(4):
            pay_ref[y * 4 + y_lo, :DATA, :] = total[y_lo * DATA : (y_lo + 1) * DATA].astype(jnp.bfloat16)
            pay_ref[y * 4 + y_lo, DATA:, :] = rows


def middle(*args):
    return pl.pallas_call(
        middle_kernel,
        out_shape=jax.ShapeDtypeStruct((8, DATA + CARRY, 128), jnp.bfloat16),
        in_specs=[whole()] * len(args),
        out_specs=whole(),
        compiler_params=pltpu.CompilerParams(vmem_limit_bytes=SMALL_LIMIT),
        name="middle",
    )(*args)


def close_kernel(got_ref, energy_ref, gradient_ref):
    escale = 1.0 / (NCHOL * NOCC)
    gscale = 1.0 / NCHOL**0.5
    total = got_ref[0].astype(jnp.float32)
    for n in range(1, 8):
        total = total + got_ref[n].astype(jnp.float32)
    for w in range(WPER):
        rest = total[2 * BLOCK : DATA, 64 * w : 64 * (w + 1)]
        gradient_ref[w] = jnp.concatenate([total[BLOCK * w : BLOCK * (w + 1)], rest], axis=1) * gscale
        energy_ref[w] = carried(total[DATA:], w)[0, 0] * escale


def close(got):
    return pl.pallas_call(
        close_kernel,
        out_shape=(
            jax.ShapeDtypeStruct((WPER,), jnp.float32),
            jax.ShapeDtypeStruct((WPER, BLOCK, NOCC), jnp.float32),
        ),
        in_specs=[whole()],
        out_specs=(pl.BlockSpec(memory_space=pltpu.SMEM), whole()),
        compiler_params=pltpu.CompilerParams(vmem_limit_bytes=SMALL_LIMIT),
        name="close",
    )(got)


def swap(value, axis):
    return lax.ppermute(value, axis, [(0, 1), (1, 0)])


def exchange(value, axes):
    return lax.all_to_all(value, axes, split_axis=0, concat_axis=0, tiled=True)


def per_device(chol_vectors, green):
    turned = jnp.swapaxes(green, 1, 2).reshape(WPER * NOCC, M)
    share = lax.dynamic_index_in_dim(turned.reshape(4, SHARE, M), lax.axis_index("x"), 0, keepdims=False)
    packed = exchange(chol_vectors.reshape(4, QUARTER, ROWS, NOCC), ("y_hi", "core"))
    packed, share = lax.optimization_barrier((packed, share))
    share = swap(share, "y_hi")
    other = lax.all_gather(share, "x", axis=0, tiled=True)
    own = exchange(fan(packed), "z")
    own, other = lax.optimization_barrier((own, other))
    sib = swap(own, "core")
    own, sib = (value.reshape(8, 2, BLOCK, CHUNK) for value in (own, sib))
    stack0, e0 = products(turned, other, own)
    stack1, e1 = products(turned, other, sib)
    got = exchange(middle(exchange(spread(own, sib, stack0, stack1, e0, e1), "x")), ("y_hi", "y_lo"))
    return close(got)


def solution(mesh):
    torus = Mesh(
        mesh.devices.reshape(2, 8, 2, 4, 4),
        ("y_hi", "z", "core", "y_lo", "x"),
    )
    return jax.shard_map(
        per_device,
        mesh=torus,
        in_specs=(P(CHOL, WALKER, None), P(WALKER, None, None)),
        out_specs=(P(WALKER), P(WALKER, CHOL, None)),
        check_vma=False,
    )
```

```python
import jax
import jax.numpy as jnp
from jax import lax
from jax.experimental import pallas as pl
from jax.experimental.pallas import tpu as pltpu
from jax.sharding import Mesh
from jax.sharding import PartitionSpec as P

M = 768
NOCC = 192
NCHOL = 256
WALKER = ("y_hi", "z", "core")
CHOL = ("y_lo", "x")
ROWS = 24
BLOCK = 2 * ROWS
WPER = 2
QUARTER = 4
CHUNK = QUARTER * NOCC
SHARE = WPER * NOCC // 4
NWALK = 2 * WPER
DATA = 3 * BLOCK
CARRY = 16
VMEM_LIMIT = 32 * 1024 * 1024
SMALL_LIMIT = 16 * 1024 * 1024


def whole():
    return pl.BlockSpec(memory_space=pltpu.VMEM)


def fan_kernel(in_ref, out_ref):
    for n in range(4):
        for k in range(0, QUARTER, 2):
            pair = jnp.concatenate([in_ref[n, k], in_ref[n, k + 1]], axis=1)
            for z in range(8):
                out_ref[z, n, :, k * NOCC : (k + 2) * NOCC] = pair


def fan(quarters):
    return pl.pallas_call(
        fan_kernel,
        out_shape=jax.ShapeDtypeStruct((8, 4, ROWS, CHUNK), jnp.bfloat16),
        in_specs=[whole()],
        out_specs=whole(),
        compiler_params=pltpu.CompilerParams(vmem_limit_bytes=SMALL_LIMIT),
        name="fan",
    )(quarters)


def split3(value):
    high = value.astype(jnp.bfloat16).astype(jnp.float32)
    left = value - high
    mid = left.astype(jnp.bfloat16).astype(jnp.float32)
    return high, mid, left - mid


def carry(values):
    row = lax.broadcasted_iota(jnp.int32, (CARRY, 128), 0)
    out = jnp.zeros((CARRY, 128), jnp.float32)
    for n, value in enumerate(values):
        filled = jnp.broadcast_to(value, (CARRY, 128))
        for p, part in enumerate(split3(filled)):
            out = jnp.where(row == 3 * n + p, part, out)
    return out.astype(jnp.bfloat16)


def carried(rows, n):
    return rows[3 * n : 3 * n + 1] + rows[3 * n + 1 : 3 * n + 2] + rows[3 * n + 2 : 3 * n + 3]


def contract(greens, x_ref, stack_ref, energy_ref):
    half = M // 2
    x = jnp.concatenate([x_ref[:, side].reshape(half, CHUNK) for side in range(2)], axis=0)
    diagonal = lax.broadcasted_iota(jnp.int32, (NOCC, NOCC), 0) == lax.broadcasted_iota(jnp.int32, (NOCC, NOCC), 1)
    greens = jnp.concatenate([green[...] for green in greens], axis=0)
    part = jnp.dot(greens, x, preferred_element_type=jnp.float32)
    for n in range(NWALK):
        walker = part[n * NOCC : (n + 1) * NOCC]
        for q in range(QUARTER):
            stack_ref[n, q * NOCC : (q + 1) * NOCC, :] = walker[:, q * NOCC : (q + 1) * NOCC].astype(jnp.bfloat16)
        trace = jnp.dot(walker.astype(jnp.bfloat16), stack_ref[n], preferred_element_type=jnp.float32)
        value = jnp.sum(jnp.where(diagonal, trace, 0.0))
        energy_ref[n : n + 1, :] = jnp.full((1, 128), value, jnp.float32)


def products_kernel(mine_ref, other_ref, x_ref, stack_ref, energy_ref):
    contract((mine_ref, other_ref), x_ref, stack_ref, energy_ref)


def params():
    return pltpu.CompilerParams(vmem_limit_bytes=VMEM_LIMIT)


STACKED = (
    jax.ShapeDtypeStruct((NWALK, CHUNK, NOCC), jnp.bfloat16),
    jax.ShapeDtypeStruct((NWALK, 128), jnp.float32),
)


def products(*args):
    return pl.pallas_call(
        products_kernel,
        out_shape=STACKED,
        in_specs=[whole()] * len(args),
        out_specs=(whole(),) * 2,
        compiler_params=params(),
        name="products",
    )(*args)


def spread_kernel(mine_ref, other_ref, own_ref, sib_ref, stack0_ref, e0_ref, pay_ref, stack1_ref, e1_ref):
    contract((mine_ref, other_ref), sib_ref, stack1_ref, e1_ref)
    side = lax.axis_index("y_hi")
    half = M // 2
    energies = e0_ref[...] + e1_ref[...]
    for g in range(2):
        y = side if g == 0 else 1 - side
        for m in range(2):
            grads = []
            for w in range(WPER):
                n = g * WPER + w
                grad = jnp.dot(own_ref[:, m].reshape(half, CHUNK), stack0_ref[n], preferred_element_type=jnp.float32)
                grads.append(
                    grad + jnp.dot(sib_ref[:, m].reshape(half, CHUNK), stack1_ref[n], preferred_element_type=jnp.float32)
                )
            rest = jnp.concatenate([grads[0][:, 128:], grads[1][:, 128:]], axis=1).astype(jnp.bfloat16)
            parts = [grad[:, :128].astype(jnp.bfloat16) for grad in grads] + [rest]
            for b in range(8):
                x, y_lo = b % 4, m * 2 + b // 4
                for p, part in enumerate(parts):
                    base = y_lo * DATA + p * BLOCK
                    pay_ref[x, y, base : base + BLOCK, :] = part[b * BLOCK : (b + 1) * BLOCK]
        rows = carry([energies[g * WPER + w : g * WPER + w + 1, :1] for w in range(WPER)])
        for x in range(4):
            pay_ref[x, y, 4 * DATA : 4 * DATA + CARRY, :] = rows


def spread(*args):
    return pl.pallas_call(
        spread_kernel,
        out_shape=jax.ShapeDtypeStruct((4, 2, 4 * DATA + CARRY, 128), jnp.bfloat16),
        in_specs=[whole()] * len(args),
        out_specs=whole(),
        scratch_shapes=[pltpu.VMEM(shape.shape, shape.dtype) for shape in STACKED],
        compiler_params=params(),
        name="spread",
    )(*args)


def middle_kernel(got_ref, pay_ref):
    for y in range(2):
        total = got_ref[0, y].astype(jnp.float32)
        for x in range(1, 4):
            total = total + got_ref[x, y].astype(jnp.float32)
        rows = carry([carried(total[4 * DATA :], w)[:, :1] for w in range(WPER)])
        for y_lo in range(4):
            pay_ref[y * 4 + y_lo, :DATA, :] = total[y_lo * DATA : (y_lo + 1) * DATA].astype(jnp.bfloat16)
            pay_ref[y * 4 + y_lo, DATA:, :] = rows


def middle(*args):
    return pl.pallas_call(
        middle_kernel,
        out_shape=jax.ShapeDtypeStruct((8, DATA + CARRY, 128), jnp.bfloat16),
        in_specs=[whole()] * len(args),
        out_specs=whole(),
        compiler_params=pltpu.CompilerParams(vmem_limit_bytes=SMALL_LIMIT),
        name="middle",
    )(*args)


def close_kernel(got_ref, energy_ref, gradient_ref):
    escale = 1.0 / (NCHOL * NOCC)
    gscale = 1.0 / NCHOL**0.5
    total = got_ref[0].astype(jnp.float32)
    for n in range(1, 8):
        total = total + got_ref[n].astype(jnp.float32)
    for w in range(WPER):
        rest = total[2 * BLOCK : DATA, 64 * w : 64 * (w + 1)]
        gradient_ref[w] = jnp.concatenate([total[BLOCK * w : BLOCK * (w + 1)], rest], axis=1) * gscale
        energy_ref[w] = carried(total[DATA:], w)[0, 0] * escale


def close(got):
    return pl.pallas_call(
        close_kernel,
        out_shape=(
            jax.ShapeDtypeStruct((WPER,), jnp.float32),
            jax.ShapeDtypeStruct((WPER, BLOCK, NOCC), jnp.float32),
        ),
        in_specs=[whole()],
        out_specs=(pl.BlockSpec(memory_space=pltpu.SMEM), whole()),
        compiler_params=pltpu.CompilerParams(vmem_limit_bytes=SMALL_LIMIT),
        name="close",
    )(got)


def swap(value, axis):
    return lax.ppermute(value, axis, [(0, 1), (1, 0)])


def exchange(value, axes):
    return lax.all_to_all(value, axes, split_axis=0, concat_axis=0, tiled=True)


def per_device(chol_vectors, green):
    turned = jnp.swapaxes(green, 1, 2).reshape(WPER * NOCC, M)
    share = lax.dynamic_index_in_dim(turned.reshape(4, SHARE, M), lax.axis_index("x"), 0, keepdims=False)
    packed = exchange(chol_vectors.reshape(4, QUARTER, ROWS, NOCC), ("y_hi", "core"))
    packed, share = lax.optimization_barrier((packed, share))
    share = swap(share, "y_hi")
    other = lax.all_gather(share, "x", axis=0, tiled=True)
    own = exchange(fan(packed), "z")
    own, other = lax.optimization_barrier((own, other))
    sib = swap(own, "core")
    own, sib = (value.reshape(8, 2, BLOCK, CHUNK) for value in (own, sib))
    stack0, e0 = products(turned, other, own)
    got = exchange(middle(exchange(spread(turned, other, own, sib, stack0, e0), "x")), ("y_hi", "y_lo"))
    return close(got)


def solution(mesh):
    torus = Mesh(
        mesh.devices.reshape(2, 8, 2, 4, 4),
        ("y_hi", "z", "core", "y_lo", "x"),
    )
    return jax.shard_map(
        per_device,
        mesh=torus,
        in_specs=(P(CHOL, WALKER, None), P(WALKER, None, None)),
        out_specs=(P(WALKER), P(WALKER, CHOL, None)),
        check_vma=False,
    )
```

```python
import jax
import jax.numpy as jnp
from jax import lax
from jax.experimental import pallas as pl
from jax.experimental.pallas import tpu as pltpu
from jax.sharding import Mesh
from jax.sharding import PartitionSpec as P

M = 768
NOCC = 192
NCHOL = 256
WALKER = ("y_hi", "z", "core")
CHOL = ("y_lo", "x")
ROWS = 24
BLOCK = 2 * ROWS
WPER = 2
QUARTER = 4
CHUNK = QUARTER * NOCC
SHARE = WPER * NOCC // 4
NWALK = 2 * WPER
DATA = 3 * BLOCK
CARRY = 16
VMEM_LIMIT = 32 * 1024 * 1024
SMALL_LIMIT = 16 * 1024 * 1024


def whole():
    return pl.BlockSpec(memory_space=pltpu.VMEM)


def fan_kernel(in_ref, out_ref):
    for n in range(4):
        for k in range(0, QUARTER, 2):
            pair = jnp.concatenate([in_ref[n, k], in_ref[n, k + 1]], axis=1)
            for z in range(8):
                out_ref[z, n, :, k * NOCC : (k + 2) * NOCC] = pair


def fan(quarters):
    return pl.pallas_call(
        fan_kernel,
        out_shape=jax.ShapeDtypeStruct((8, 4, ROWS, CHUNK), jnp.bfloat16),
        in_specs=[whole()],
        out_specs=whole(),
        compiler_params=pltpu.CompilerParams(vmem_limit_bytes=SMALL_LIMIT),
        name="fan",
    )(quarters)


def split3(value):
    high = value.astype(jnp.bfloat16).astype(jnp.float32)
    left = value - high
    mid = left.astype(jnp.bfloat16).astype(jnp.float32)
    return high, mid, left - mid


def carry(values):
    row = lax.broadcasted_iota(jnp.int32, (CARRY, 128), 0)
    out = jnp.zeros((CARRY, 128), jnp.float32)
    for n, value in enumerate(values):
        filled = jnp.broadcast_to(value, (CARRY, 128))
        for p, part in enumerate(split3(filled)):
            out = jnp.where(row == 3 * n + p, part, out)
    return out.astype(jnp.bfloat16)


def carried(rows, n):
    return rows[3 * n : 3 * n + 1] + rows[3 * n + 1 : 3 * n + 2] + rows[3 * n + 2 : 3 * n + 3]


def contract(greens, x_ref, stack_ref, energy_ref):
    half = M // 2
    x = jnp.concatenate([x_ref[:, side].reshape(half, CHUNK) for side in range(2)], axis=0)
    diagonal = lax.broadcasted_iota(jnp.int32, (NOCC, NOCC), 0) == lax.broadcasted_iota(jnp.int32, (NOCC, NOCC), 1)
    greens = jnp.concatenate([green[...] for green in greens], axis=0)
    part = jnp.dot(greens, x, preferred_element_type=jnp.float32)
    for n in range(NWALK):
        walker = part[n * NOCC : (n + 1) * NOCC]
        for q in range(QUARTER):
            stack_ref[n, q * NOCC : (q + 1) * NOCC, :] = walker[:, q * NOCC : (q + 1) * NOCC].astype(jnp.bfloat16)
        trace = jnp.dot(walker.astype(jnp.bfloat16), stack_ref[n], preferred_element_type=jnp.float32)
        value = jnp.sum(jnp.where(diagonal, trace, 0.0))
        energy_ref[n : n + 1, :] = jnp.full((1, 128), value, jnp.float32)


def products_kernel(mine_ref, other_ref, x_ref, stack_ref, energy_ref):
    contract((mine_ref, other_ref), x_ref, stack_ref, energy_ref)


def params():
    return pltpu.CompilerParams(vmem_limit_bytes=VMEM_LIMIT)


STACKED = (
    jax.ShapeDtypeStruct((NWALK, CHUNK, NOCC), jnp.bfloat16),
    jax.ShapeDtypeStruct((NWALK, 128), jnp.float32),
)


def products(*args):
    return pl.pallas_call(
        products_kernel,
        out_shape=STACKED,
        in_specs=[whole()] * len(args),
        out_specs=(whole(),) * 2,
        compiler_params=params(),
        name="products",
    )(*args)


def spread_kernel(mine_ref, other_ref, own_ref, sib_ref, stack0_ref, e0_ref, pay_ref, stack1_ref, e1_ref):
    contract((mine_ref, other_ref), sib_ref, stack1_ref, e1_ref)
    side = lax.axis_index("y_hi")
    half = M // 2
    energies = e0_ref[...] + e1_ref[...]
    for g in range(2):
        y = side if g == 0 else 1 - side
        for m in range(2):
            grads = []
            for w in range(WPER):
                n = g * WPER + w
                grad = jnp.dot(own_ref[:, m].reshape(half, CHUNK), stack0_ref[n], preferred_element_type=jnp.float32)
                grads.append(
                    grad + jnp.dot(sib_ref[:, m].reshape(half, CHUNK), stack1_ref[n], preferred_element_type=jnp.float32)
                )
            rest = jnp.concatenate([grads[0][:, 128:], grads[1][:, 128:]], axis=1).astype(jnp.bfloat16)
            parts = [grad[:, :128].astype(jnp.bfloat16) for grad in grads] + [rest]
            for b in range(8):
                x, y_lo = b % 4, m * 2 + b // 4
                for p, part in enumerate(parts):
                    base = y_lo * DATA + p * BLOCK
                    pay_ref[x, y, base : base + BLOCK, :] = part[b * BLOCK : (b + 1) * BLOCK]
        rows = carry([energies[g * WPER + w : g * WPER + w + 1, :1] for w in range(WPER)])
        for x in range(4):
            pay_ref[x, y, 4 * DATA : 4 * DATA + CARRY, :] = rows


def spread(*args):
    return pl.pallas_call(
        spread_kernel,
        out_shape=jax.ShapeDtypeStruct((4, 2, 4 * DATA + CARRY, 128), jnp.bfloat16),
        in_specs=[whole()] * len(args),
        out_specs=whole(),
        scratch_shapes=[pltpu.VMEM(shape.shape, shape.dtype) for shape in STACKED],
        compiler_params=params(),
        name="spread",
    )(*args)


def middle_kernel(got_ref, pay_ref):
    for y in range(2):
        total = got_ref[0, y].astype(jnp.float32)
        for x in range(1, 4):
            total = total + got_ref[x, y].astype(jnp.float32)
        rows = carry([carried(total[4 * DATA :], w)[:, :1] for w in range(WPER)])
        for y_lo in range(4):
            pay_ref[y * 4 + y_lo, :DATA, :] = total[y_lo * DATA : (y_lo + 1) * DATA].astype(jnp.bfloat16)
            pay_ref[y * 4 + y_lo, DATA:, :] = rows


def middle(*args):
    return pl.pallas_call(
        middle_kernel,
        out_shape=jax.ShapeDtypeStruct((8, DATA + CARRY, 128), jnp.bfloat16),
        in_specs=[whole()] * len(args),
        out_specs=whole(),
        compiler_params=pltpu.CompilerParams(vmem_limit_bytes=SMALL_LIMIT),
        name="middle",
    )(*args)


def close_kernel(got_ref, energy_ref, gradient_ref):
    escale = 1.0 / (NCHOL * NOCC)
    gscale = 1.0 / NCHOL**0.5
    total = got_ref[0].astype(jnp.float32)
    for n in range(1, 8):
        total = total + got_ref[n].astype(jnp.float32)
    for w in range(WPER):
        rest = total[2 * BLOCK : DATA, 64 * w : 64 * (w + 1)]
        gradient_ref[w] = jnp.concatenate([total[BLOCK * w : BLOCK * (w + 1)], rest], axis=1) * gscale
        energy_ref[w] = carried(total[DATA:], w)[0, 0] * escale


def close(got):
    return pl.pallas_call(
        close_kernel,
        out_shape=(
            jax.ShapeDtypeStruct((WPER,), jnp.float32),
            jax.ShapeDtypeStruct((WPER, BLOCK, NOCC), jnp.float32),
        ),
        in_specs=[whole()],
        out_specs=(pl.BlockSpec(memory_space=pltpu.SMEM), whole()),
        compiler_params=pltpu.CompilerParams(vmem_limit_bytes=SMALL_LIMIT),
        name="close",
    )(got)


def swap(value, axis):
    return lax.ppermute(value, axis, [(0, 1), (1, 0)])


def exchange(value, axes):
    return lax.all_to_all(value, axes, split_axis=0, concat_axis=0, tiled=True)


def per_device(chol_vectors, green):
    turned = jnp.swapaxes(green, 1, 2).reshape(WPER * NOCC, M)
    share = lax.dynamic_index_in_dim(turned.reshape(4, SHARE, M), lax.axis_index("x"), 0, keepdims=False)
    packed = exchange(chol_vectors.reshape(4, QUARTER, ROWS, NOCC), ("y_hi", "core"))
    share = swap(share, "y_hi")
    other = lax.all_gather(share, "x", axis=0, tiled=True)
    own = exchange(fan(packed), "z")
    own, other = lax.optimization_barrier((own, other))
    sib = swap(own, "core")
    own, sib = (value.reshape(8, 2, BLOCK, CHUNK) for value in (own, sib))
    stack0, e0 = products(turned, other, own)
    got = exchange(middle(exchange(spread(turned, other, own, sib, stack0, e0), "x")), ("y_hi", "y_lo"))
    return close(got)


def solution(mesh):
    torus = Mesh(
        mesh.devices.reshape(2, 8, 2, 4, 4),
        ("y_hi", "z", "core", "y_lo", "x"),
    )
    return jax.shard_map(
        per_device,
        mesh=torus,
        in_specs=(P(CHOL, WALKER, None), P(WALKER, None, None)),
        out_specs=(P(WALKER), P(WALKER, CHOL, None)),
        check_vma=False,
    )
```
